128 devices in a mesh: sink: 8 (over x, z_hi), src: 16 (over z_lo, y, core).
Axes of the slice: x: 4, y: 4, z: 4 (z_hi: 2, z_lo: 2; z = z_hi * 2 + z_lo), core: 2. Of those that a mesh axis runs over, the one named last changes fastest.
Arguments:
- perambulator: bfloat16 [2, 16, 32, 512, 512], P(None, None, 'src', None, 'sink'), may hold values from -6 to 6
- elementals: bfloat16 [2, 16, 8, 512, 512], P(None, 'sink', None, 'src'), may hold values from -0.1875 to 0.1875
- op_ids: int32 [16, 8], P('sink'), may hold values from 0 to 7, each once within a row
Outputs:
- products: bfloat16 [2, 4, 16, 32, 512, 512], P(None, None, 'sink', 'src')
The draws below stay inside these ranges and needn't reach their ends.
Inputs may be any that keep to these rules, and one draw needn't show every extreme that they name: `op_ids`: each row is a permutation of 0 to 7.
All inputs are finite; a program needn't handle non-finite values.
Results may differ from the reference program's by a relative error of at most 0.001.
Values may be sent and summed in bfloat16 or wider, within the bound.
A program may use at most 128 MiB of HBM per device.

```python
import jax
import jax.numpy as jnp
from jax import lax

NV = 512
NOP = 4
NBANK = 8
SINKT = 16
SRCT = 32


def block_scale(rng, extent, shards, least, largest):
    level, own = 1.0, jax.random.fold_in(rng, 6)
    for axis_at, shards_of in shards:
        steps = jnp.exp(jax.random.uniform(jax.random.fold_in(own, axis_at), (shards_of,), jnp.float32, least / len(shards), largest / len(shards)))
        level = level * jnp.repeat(steps, extent[axis_at] // shards_of).reshape([-1 if axis == axis_at else 1 for axis in range(len(extent))])
    return level


def gaussian(stream_key, dims, deviation, most, split=(), held_as=jnp.bfloat16):
    array = deviation * jax.random.normal(stream_key, dims, jnp.float32)
    if split:
        array = array * block_scale(stream_key, dims, split, -0.22, 0.18)
    return jnp.clip(array, -most, most).astype(held_as)


def setup_inputs(seed: int = 0) -> dict:
    arg_keys = jax.random.split(jax.random.key(seed), 4)
    return {
        "perambulator": gaussian(arg_keys[0], (2, SINKT, SRCT, NV, NV), 1.0, 6.0, ((2, 16), (4, 8))),
        "elementals": gaussian(arg_keys[1], (2, SINKT, NBANK, NV, NV), (2 * NV) ** -0.5, 0.1875, ((1, 8), (3, 16))),
        "op_ids": jax.vmap(lambda own: jax.random.permutation(own, NBANK))(jax.random.split(arg_keys[2], SINKT)).reshape((SINKT, NBANK)).astype(jnp.int32),
    }


def one_time(args):
    peram, bank, ids = args
    chosen = jnp.take(bank, ids[:NOP], axis=1).astype(jnp.float32)
    peram = peram.astype(jnp.float32)
    real_part = jnp.einsum("orv,svw->osrw", chosen[0], peram[0]) - jnp.einsum("orv,svw->osrw", chosen[1], peram[1])
    imag_part = jnp.einsum("orv,svw->osrw", chosen[0], peram[1]) + jnp.einsum("orv,svw->osrw", chosen[1], peram[0])
    return jnp.stack([real_part, imag_part]).astype(jnp.bfloat16)


def reference(perambulator, elementals, op_ids):
    peram_t = jnp.moveaxis(perambulator, 1, 0)
    bank_t = jnp.moveaxis(elementals, 1, 0)
    result = lax.map(one_time, (peram_t, bank_t, op_ids))
    return jnp.moveaxis(result, 0, 3).transpose(0, 1, 3, 2, 4, 5)
```

```python
import functools

import jax
import jax.numpy as jnp
from jax import lax
from jax.experimental import pallas as pl
from jax.experimental.pallas import tpu as pltpu
from jax.sharding import PartitionSpec as P

NOP = 4
MESH = pl.DeviceIdType.MESH
HOPS = ((1, 0), (3, 0), (0, 1), (2, 0), (1, 1), (3, 1), (2, 1))
BF16 = jnp.bfloat16


def kernel(ids, stored, peram, out, bank, ops, cols, weights, load_sem, own_sem, p_send, p_recv, z_send, z_recv, y_send, y_recv, c_send, c_recv):
    sink, src = lax.axis_index("sink"), lax.axis_index("src")
    x, zh = sink // 2, sink % 2
    zl, y, core = src // 8, (src // 2) % 4, src % 2

    def sink_of(dx, dz):
        return lax.rem(x + dx, 4) * 2 + lax.rem(zh + dz, 2)

    def src_of(dl, dy, dc):
        return lax.rem(zl + dl, 2) * 8 + lax.rem(y + dy, 4) * 2 + lax.rem(core + dc, 2)

    load = pltpu.make_async_copy(stored, bank, load_sem)
    load.start()

    barrier = pltpu.get_barrier_semaphore()
    partners = [(sink_of(dx, dz), src) for dx, dz in HOPS]
    partners += [(sink, src_of(0, dy, 0)) for dy in (1, 2, 3)]
    partners += [(sink, src_of(1, 0, 0)), (sink, src_of(0, 0, 1))]
    for partner in partners:
        pl.semaphore_signal(barrier, inc=1, device_id=partner, device_id_type=MESH)

    load.wait()
    rows = pl.ds(pl.multiple_of(src * 32, 32), 32)
    for t in range(2):
        for o in range(NOP):
            which = ids[t, o]
            for c in range(2):
                ops[t, o, rows, c * 512 : (c + 1) * 512] = bank[c, t, which]

    pl.semaphore_wait(barrier, len(partners))

    def rows_of(block):
        return pl.ds(pl.multiple_of(block * 32, 32), 32)

    def op_copy(block, t, send, recv, target):
        piece = ops.at[t, :, rows_of(block), :]
        return pltpu.make_async_remote_copy(
            src_ref=piece, dst_ref=piece, send_sem=send, recv_sem=recv, device_id=(sink, target), device_id_type=MESH
        )

    def z_copy(t, arriving=False):
        return op_copy(src_of(1, 0, 0) if arriving else src, t, z_send.at[t], z_recv.at[t], src_of(1, 0, 0))

    def y_copy(h, dy, t, arriving=False):
        block = src_of(h, 4 - dy, 0) if arriving else src_of(h, 0, 0)
        return op_copy(block, t, y_send.at[h, dy - 1, t], y_recv.at[h, dy - 1, t], src_of(0, dy, 0))

    def c_copy(h, dy, t, arriving=False):
        block = src_of(h, 4 - dy, 1 if arriving else 0)
        return op_copy(block, t, c_send.at[h, dy, t], c_recv.at[h, dy, t], src_of(0, 0, 1))

    def p_copy(k, t, s, arriving=False):
        dx, dz = HOPS[k]
        target = sink_of(dx, dz)
        owner = sink_of(4 - dx, dz) if arriving else sink
        return pltpu.make_async_remote_copy(
            src_ref=peram.at[:, 2 * target + t, s],
            dst_ref=cols.at[t, s, :, pl.ds(pl.multiple_of(owner * 64, 64), 64), :],
            send_sem=p_send.at[k, t, s],
            recv_sem=p_recv.at[k, t, s],
            device_id=(target, src),
            device_id_type=MESH,
        )

    def own_copy(t, s):
        return pltpu.make_async_copy(
            peram.at[:, 2 * sink + t, s],
            cols.at[t, s, :, pl.ds(pl.multiple_of(sink * 64, 64), 64), :],
            own_sem.at[t, s],
        )

    for t in range(2):
        z_copy(t).start()
    for t in range(2):
        for dy in (1, 3, 2):
            y_copy(0, dy, t).start()
        c_copy(0, 0, t).start()
    for t in range(2):
        for s in range(2):
            for k in range(7):
                p_copy(k, t, s).start()
            own_copy(t, s).start()

    for t in range(2):
        z_copy(t, True).wait_recv()
        for dy in (1, 3, 2):
            y_copy(1, dy, t).start()
        c_copy(1, 0, t).start()
    for h in range(2):
        for t in range(2):
            for dy in (1, 3, 2):
                y_copy(h, dy, t, True).wait_recv()
                c_copy(h, dy, t).start()
    for h in range(2):
        for t in range(2):
            for dy in range(4):
                c_copy(h, dy, t, True).wait_recv()

    def products(t, s, dx):
        first = pl.multiple_of(lax.rem(x + dx, 4) * 128, 128)
        real, imag = cols[t, s, 0, pl.ds(first, 128), :], cols[t, s, 1, pl.ds(first, 128), :]
        weights[0:128, 0:512] = real
        weights[0:128, 512:1024] = -imag
        weights[128:256, 0:512] = imag
        weights[128:256, 512:1024] = real

        def one(o, carry):
            both = lax.dot_general(
                ops[t, o], weights[...], (((1,), (1,)), ((), ())), preferred_element_type=jnp.float32
            ).astype(BF16)
            out[0, o, t, s, :, pl.ds(first, 128)] = both[:, 0:128]
            out[1, o, t, s, :, pl.ds(first, 128)] = both[:, 128:256]
            return carry

        lax.fori_loop(0, NOP, one, 0)

    for t in range(2):
        for s in range(2):
            for dx in (0, 3, 1, 2):
                for k, hop in enumerate(HOPS):
                    if hop[0] == (4 - dx) % 4:
                        p_copy(k, t, s, True).wait_recv()
                if dx == 0:
                    own_copy(t, s).wait()
                products(t, s, dx)

    for t in range(2):
        z_copy(t).wait_send()
        for h in range(2):
            for dy in range(1, 4):
                y_copy(h, dy, t).wait_send()
            for dy in range(4):
                c_copy(h, dy, t).wait_send()
        for s in range(2):
            for k in range(7):
                p_copy(k, t, s).wait_send()


def shards(perambulator, elementals, op_ids):
    peram = jnp.swapaxes(perambulator, 3, 4)
    dma = pltpu.SemaphoreType.DMA
    return pl.pallas_call(
        kernel,
        out_shape=pltpu.VMEM((2, NOP, 2, 2, 512, 512), BF16),
        in_specs=[
            pl.BlockSpec(memory_space=pltpu.SMEM),
            pl.BlockSpec(memory_space=pl.ANY),
            pl.BlockSpec(memory_space=pl.ANY),
        ],
        out_specs=pl.BlockSpec(memory_space=pltpu.VMEM),
        scratch_shapes=[
            pltpu.VMEM((2, 2, 8, 32, 512), BF16),
            pltpu.VMEM((2, NOP, 512, 1024), BF16),
            pltpu.VMEM((2, 2, 2, 512, 512), BF16),
            pltpu.VMEM((256, 1024), BF16),
            dma(()),
            dma((2, 2)),
            dma((7, 2, 2)),
            dma((7, 2, 2)),
            dma((2,)),
            dma((2,)),
            dma((2, 3, 2)),
            dma((2, 3, 2)),
            dma((2, 4, 2)),
            dma((2, 4, 2)),
        ],
        compiler_params=pltpu.CompilerParams(
            collective_id=0, has_side_effects=True, vmem_limit_bytes=40 * 2**20
        ),
    )(op_ids, elementals, peram)


def solution(mesh):
    in_specs = (
        P(None, None, "src", None, "sink"),
        P(None, "sink", None, "src", None),
        P("sink", None),
    )
    out_specs = P(None, None, "sink", "src", None, None)
    return jax.shard_map(shards, mesh=mesh, in_specs=in_specs, out_specs=out_specs, check_vma=False)
```

```python
import functools

import jax
import jax.numpy as jnp
from jax import lax
from jax.experimental import pallas as pl
from jax.experimental.pallas import tpu as pltpu
from jax.sharding import PartitionSpec as P

NOP = 4
MESH = pl.DeviceIdType.MESH
BF16 = jnp.bfloat16


def kernel(ids, stored, peram, out, ops, cols, bank, weights, load_sem, p_send, p_recv, z_send, z_recv, y_send, y_recv, f_send, f_recv, c_send, c_recv):
    sink, src = lax.axis_index("sink"), lax.axis_index("src")
    x, zh = sink // 2, sink % 2
    zl, y, core = src // 8, (src // 2) % 4, src % 2

    def sink_of(dx, dz):
        return lax.rem(x + dx, 4) * 2 + lax.rem(zh + dz, 2)

    def src_of(dl, dy, dc):
        return lax.rem(zl + dl, 2) * 8 + lax.rem(y + dy, 4) * 2 + lax.rem(core + dc, 2)

    load = pltpu.make_async_copy(stored, bank, load_sem)
    load.start()

    barrier = pltpu.get_barrier_semaphore()
    partners = [(sink_of(dx, dz), src) for dx in range(4) for dz in range(2) if dx or dz]
    partners += [(sink, src_of(0, dy, 0)) for dy in (1, 3)]
    partners += [(sink, src_of(1, 0, 0)), (sink, src_of(0, 0, 1))]
    for partner in partners:
        pl.semaphore_signal(barrier, inc=1, device_id=partner, device_id_type=MESH)

    load.wait()
    rows = pl.ds(pl.multiple_of(src * 32, 32), 32)
    for t in range(2):
        for o in range(NOP):
            which = ids[t, o]
            for c in range(2):
                ops[t, o, rows, c * 512 : (c + 1) * 512] = bank[c, t, which]

    pl.semaphore_wait(barrier, len(partners))

    def op_copy(block, t, send, recv, target, o=slice(0, NOP)):
        piece = ops.at[t, o, pl.ds(pl.multiple_of(block * 32, 32), 32), :]
        return pltpu.make_async_remote_copy(
            src_ref=piece, dst_ref=piece, send_sem=send, recv_sem=recv, device_id=(sink, target), device_id_type=MESH
        )

    def z_copy(t, arriving=False):
        return op_copy(src_of(1, 0, 0) if arriving else src, t, z_send.at[t], z_recv.at[t], src_of(1, 0, 0))

    def y_copy(h, way, t, arriving=False):
        back, to = (3, 1) if way == 0 else (1, 3)
        block = src_of(h, back if arriving else 0, 0)
        return op_copy(block, t, y_send.at[h, way, t], y_recv.at[h, way, t], src_of(0, to, 0))

    def f_copy(h, way, t, arriving=False):
        back, to = (3, 1) if way == 0 else (1, 3)
        block = src_of(h, 2 if arriving else back, 0)
        half = slice(2 * way, 2 * way + 2)
        return op_copy(block, t, f_send.at[h, way, t], f_recv.at[h, way, t], src_of(0, to, 0), half)

    def c_copy(h, dy, t, arriving=False):
        block = src_of(h, dy, 1 if arriving else 0)
        return op_copy(block, t, c_send.at[h, dy, t], c_recv.at[h, dy, t], src_of(0, 0, 1))

    def p_copy(dx, dz, t, s, arriving=False):
        target = sink_of(dx, dz)
        owner = sink_of(4 - dx, dz) if arriving else sink
        here = peram.at[:, 2 * target + t, s]
        there = cols.at[t, s, :, pl.ds(pl.multiple_of(owner * 64, 64), 64), :]
        if not arriving and dx == 0 and dz == 0:
            return pltpu.make_async_copy(here, there, p_recv.at[0, 0, t, s])
        return pltpu.make_async_remote_copy(
            src_ref=here,
            dst_ref=there,
            send_sem=p_send.at[dx, dz, t, s],
            recv_sem=p_recv.at[dx, dz, t, s],
            device_id=(target, src),
            device_id_type=MESH,
        )

    def send_own(t):
        for way in range(2):
            y_copy(0, way, t).start()
        c_copy(0, 0, t).start()

    def send_columns(dz, t, s):
        for dx in (0, 1, 3, 2):
            p_copy(dx, dz, t, s).start()

    def pass_on(h, t):
        for way in range(2):
            y_copy(h, way, t, True).wait_recv()
            f_copy(h, way, t).start()
            c_copy(h, 3 - 2 * way, t).start()

    z_copy(0).start()
    send_own(0)
    z_copy(1).start()
    send_own(1)
    send_columns(1, 0, 0)
    send_columns(0, 0, 0)
    for t in range(2):
        z_copy(t, True).wait_recv()
        for way in range(2):
            y_copy(1, way, t).start()
        c_copy(1, 0, t).start()
        pass_on(0, t)
    send_columns(1, 0, 1)
    send_columns(0, 0, 1)
    for t in range(2):
        pass_on(1, t)
    send_columns(1, 1, 0)
    send_columns(0, 1, 0)
    for h in range(2):
        for t in range(2):
            for way in range(2):
                f_copy(h, way, t, True).wait_recv()
            c_copy(h, 2, t).start()
    send_columns(1, 1, 1)
    send_columns(0, 1, 1)
    for h in range(2):
        for t in range(2):
            for dy in range(4):
                c_copy(h, dy, t, True).wait_recv()

    def products(i, carry):
        t, s, pair = i // 4, (i // 2) % 2, i % 2
        steps = (3 * pair, 1 + pair)
        firsts = [pl.multiple_of(lax.rem(x + 4 - dx, 4) * 128, 128) for dx in steps]
        for n, dx in enumerate(steps):
            for dz in range(2):
                p_copy(dx, dz, t, s, True).wait_recv()
        for n, first in enumerate(firsts):
            real, imag = cols[t, s, 0, pl.ds(first, 128), :], cols[t, s, 1, pl.ds(first, 128), :]
            weights[256 * n : 256 * n + 128, 0:512] = real
            weights[256 * n : 256 * n + 128, 512:1024] = -imag
            weights[256 * n + 128 : 256 * n + 256, 0:512] = imag
            weights[256 * n + 128 : 256 * n + 256, 512:1024] = real
        for o in range(NOP):
            result = lax.dot_general(
                ops[t, o], weights[...], (((1,), (1,)), ((), ())), preferred_element_type=jnp.float32
            ).astype(BF16)
            for n, first in enumerate(firsts):
                for c in range(2):
                    at = 256 * n + 128 * c
                    out[c, o, t, s, :, pl.ds(first, 128)] = result[:, at : at + 128]
        return carry

    lax.fori_loop(0, 6, products, 0)

    for dx in range(4):
        for dz in range(2):
            p_copy(dx, dz, 1, 1, True).wait_recv()

    both = ((0, 0), (0, 1), (1, 0), (1, 1))
    for t in range(2):
        z_copy(t).wait_send()
        for h in range(2):
            for way in range(2):
                y_copy(h, way, t).wait_send()
                f_copy(h, way, t).wait_send()
            for dy in range(4):
                c_copy(h, dy, t).wait_send()
    for t, s in both:
        for dx in range(4):
            for dz in range(2):
                if dx or dz:
                    p_copy(dx, dz, t, s).wait_send()


def last_kernel(done, ops, cols, out, weights, result, sem):
    moves = []
    for c in range(2):
        for o in range(NOP):
            moves.append(pltpu.make_async_copy(done.at[c, o, 0], out.at[c, o, 0], sem.at[c, o, 0]))
            moves.append(pltpu.make_async_copy(done.at[c, o, 1, 0], out.at[c, o, 1, 0], sem.at[c, o, 1]))
    for move in moves:
        move.start()
    real, imag = cols[1, 1, 0], cols[1, 1, 1]
    weights[0:512, 0:512] = real
    weights[0:512, 512:1024] = -imag
    weights[512:1024, 0:512] = imag
    weights[512:1024, 512:1024] = real
    for o in range(NOP):
        for c in range(2):
            for n in range(2):
                rows = slice(512 * c + 256 * n, 512 * c + 256 * n + 256)
                result[c, o, :, 256 * n : 256 * n + 256] = lax.dot_general(
                    ops[1, o], weights[rows, :], (((1,), (1,)), ((), ())), preferred_element_type=jnp.float32
                ).astype(BF16)
            move = pltpu.make_async_copy(result.at[c, o], out.at[c, o, 1, 1], sem.at[c, o, 2])
            move.start()
            moves.append(move)
    for move in moves:
        move.wait()


def shards(perambulator, elementals, op_ids):
    peram = jnp.swapaxes(perambulator, 3, 4)
    dma = pltpu.SemaphoreType.DMA
    vmem = pl.BlockSpec(memory_space=pltpu.VMEM)
    hbm = pl.BlockSpec(memory_space=pl.ANY)
    done, ops, cols = pl.pallas_call(
        kernel,
        out_shape=(
            pltpu.VMEM((2, NOP, 2, 2, 512, 512), BF16),
            pltpu.VMEM((2, NOP, 512, 1024), BF16),
            pltpu.VMEM((2, 2, 2, 512, 512), BF16),
        ),
        in_specs=[pl.BlockSpec(memory_space=pltpu.SMEM), hbm, hbm],
        out_specs=(vmem, vmem, vmem),
        scratch_shapes=[
            pltpu.VMEM((2, 2, 8, 32, 512), BF16),
            pltpu.VMEM((512, 1024), BF16),
            dma(()),
            dma((4, 2, 2, 2)),
            dma((4, 2, 2, 2)),
            dma((2,)),
            dma((2,)),
            dma((2, 2, 2)),
            dma((2, 2, 2)),
            dma((2, 2, 2)),
            dma((2, 2, 2)),
            dma((2, 4, 2)),
            dma((2, 4, 2)),
        ],
        compiler_params=pltpu.CompilerParams(
            collective_id=0, has_side_effects=True, vmem_limit_bytes=12 * 2**20
        ),
    )(pltpu.with_memory_space_constraint(op_ids, pltpu.HBM), pltpu.with_memory_space_constraint(elementals, pltpu.HBM), pltpu.with_memory_space_constraint(peram, pltpu.HBM))
    return pl.pallas_call(
        last_kernel,
        out_shape=jax.ShapeDtypeStruct((2, NOP, 2, 2, 512, 512), BF16),
        in_specs=[vmem, vmem, vmem],
        out_specs=hbm,
        scratch_shapes=[
            pltpu.VMEM((1024, 1024), BF16),
            pltpu.VMEM((2, NOP, 512, 512), BF16),
            dma((2, NOP, 3)),
        ],
        compiler_params=pltpu.CompilerParams(vmem_limit_bytes=16 * 2**20),
    )(
        pltpu.with_memory_space_constraint(done, pltpu.VMEM),
        pltpu.with_memory_space_constraint(ops, pltpu.VMEM),
        pltpu.with_memory_space_constraint(cols, pltpu.VMEM),
    )


def solution(mesh):
    in_specs = (
        P(None, None, "src", None, "sink"),
        P(None, "sink", None, "src", None),
        P("sink", None),
    )
    out_specs = P(None, None, "sink", "src", None, None)
    return jax.shard_map(shards, mesh=mesh, in_specs=in_specs, out_specs=out_specs, check_vma=False)
```

```python
import functools

import jax
import jax.numpy as jnp
from jax import lax
from jax.experimental import pallas as pl
from jax.experimental.pallas import tpu as pltpu
from jax.sharding import PartitionSpec as P

NOP = 4
MESH = pl.DeviceIdType.MESH
HOPS = ((1, 0), (3, 0), (0, 1), (2, 0), (1, 1), (3, 1), (2, 1), (0, 0))
BF16 = jnp.bfloat16


def kernel(ids, stored, peram, out, ops, cols, bank, weights, load_sem, p_send, p_recv, z_send, z_recv, y_send, y_recv, f_send, f_recv, c_send, c_recv):
    sink, src = lax.axis_index("sink"), lax.axis_index("src")
    x, zh = sink // 2, sink % 2
    zl, y, core = src // 8, (src // 2) % 4, src % 2

    def sink_of(dx, dz):
        return lax.rem(x + dx, 4) * 2 + lax.rem(zh + dz, 2)

    def src_of(dl, dy, dc):
        return lax.rem(zl + dl, 2) * 8 + lax.rem(y + dy, 4) * 2 + lax.rem(core + dc, 2)

    load = pltpu.make_async_copy(stored, bank, load_sem)
    load.start()

    barrier = pltpu.get_barrier_semaphore()
    partners = [(sink_of(dx, dz), src) for dx in range(4) for dz in range(2) if dx or dz]
    partners += [(sink, src_of(0, dy, 0)) for dy in (1, 3)]
    partners += [(sink, src_of(1, 0, 0)), (sink, src_of(0, 0, 1))]
    for partner in partners:
        pl.semaphore_signal(barrier, inc=1, device_id=partner, device_id_type=MESH)

    load.wait()
    rows = pl.ds(pl.multiple_of(src * 32, 32), 32)
    for t in range(2):
        for o in range(NOP):
            which = ids[t, o]
            for c in range(2):
                ops[t, o, rows, c * 512 : (c + 1) * 512] = bank[c, t, which]

    pl.semaphore_wait(barrier, len(partners))

    def op_copy(block, t, send, recv, target, o=slice(0, NOP)):
        piece = ops.at[t, o, pl.ds(pl.multiple_of(block * 32, 32), 32), :]
        return pltpu.make_async_remote_copy(
            src_ref=piece, dst_ref=piece, send_sem=send, recv_sem=recv, device_id=(sink, target), device_id_type=MESH
        )

    def z_copy(t, half, arriving=False):
        block = src_of(1, 0, 0) if arriving else src
        part = slice(2 * half, 2 * half + 2)
        return op_copy(block, t, z_send.at[t, half], z_recv.at[t, half], src_of(1, 0, 0), part)

    def y_copy(h, way, t, arriving=False):
        back, to = (3, 1) if way == 0 else (1, 3)
        block = src_of(h, back if arriving else 0, 0)
        return op_copy(block, t, y_send.at[h, way, t], y_recv.at[h, way, t], src_of(0, to, 0))

    def f_copy(h, way, t, arriving=False):
        back, to = (3, 1) if way == 0 else (1, 3)
        block = src_of(h, 2 if arriving else back, 0)
        half = slice(2 * way, 2 * way + 2)
        return op_copy(block, t, f_send.at[h, way, t], f_recv.at[h, way, t], src_of(0, to, 0), half)

    def c_copy(h, dy, t, arriving=False):
        block = src_of(h, dy, 1 if arriving else 0)
        return op_copy(block, t, c_send.at[h, dy, t], c_recv.at[h, dy, t], src_of(0, 0, 1))

    def p_copy(dx, dz, t, s, arriving=False):
        target = sink_of(dx, dz)
        owner = sink_of(4 - dx, dz) if arriving else sink
        here = peram.at[:, 2 * target + t, s]
        there = cols.at[t, s, :, pl.ds(pl.multiple_of(owner * 64, 64), 64), :]
        if not arriving and dx == 0 and dz == 0:
            return pltpu.make_async_copy(here, there, p_recv.at[0, 0, t, s])
        return pltpu.make_async_remote_copy(
            src_ref=here,
            dst_ref=there,
            send_sem=p_send.at[dx, dz, t, s],
            recv_sem=p_recv.at[dx, dz, t, s],
            device_id=(target, src),
            device_id_type=MESH,
        )

    def send_own(t):
        for way in range(2):
            y_copy(0, way, t).start()
        c_copy(0, 0, t).start()

    def send_columns(t, s):
        for dx, dz in HOPS:
            p_copy(dx, dz, t, s).start()

    def pass_on(h, t):
        for way in range(2):
            y_copy(h, way, t, True).wait_recv()
            f_copy(h, way, t).start()
            c_copy(h, 3 - 2 * way, t).start()

    z_copy(0, 0).start()
    z_copy(0, 1).start()
    send_own(0)
    z_copy(1, 0).start()
    z_copy(1, 1).start()
    send_own(1)
    send_columns(0, 0)
    for t in range(2):
        z_copy(t, 0, True).wait_recv()
        z_copy(t, 1, True).wait_recv()
        for way in range(2):
            y_copy(1, way, t).start()
        c_copy(1, 0, t).start()
        pass_on(0, t)
    send_columns(0, 1)
    for t in range(2):
        pass_on(1, t)
    send_columns(1, 0)
    for h in range(2):
        for t in range(2):
            for way in range(2):
                f_copy(h, way, t, True).wait_recv()
            c_copy(h, 2, t).start()
    send_columns(1, 1)
    for h in range(2):
        for t in range(2):
            for dy in range(4):
                c_copy(h, dy, t, True).wait_recv()

    def products(i, carry):
        t, s, pair = i // 4, (i // 2) % 2, i % 2
        steps = (3 * pair, 1 + pair)
        firsts = [pl.multiple_of(lax.rem(x + 4 - dx, 4) * 128, 128) for dx in steps]
        for n, dx in enumerate(steps):
            for dz in range(2):
                p_copy(dx, dz, t, s, True).wait_recv()
        for n, first in enumerate(firsts):
            real, imag = cols[t, s, 0, pl.ds(first, 128), :], cols[t, s, 1, pl.ds(first, 128), :]
            weights[256 * n : 256 * n + 128, 0:512] = real
            weights[256 * n : 256 * n + 128, 512:1024] = -imag
            weights[256 * n + 128 : 256 * n + 256, 0:512] = imag
            weights[256 * n + 128 : 256 * n + 256, 512:1024] = real
        for o in range(NOP):
            result = lax.dot_general(
                ops[t, o], weights[...], (((1,), (1,)), ((), ())), preferred_element_type=jnp.float32
            ).astype(BF16)
            for n, first in enumerate(firsts):
                for c in range(2):
                    at = 256 * n + 128 * c
                    out[c, o, t, s, :, pl.ds(first, 128)] = result[:, at : at + 128]
        return carry

    lax.fori_loop(0, 6, products, 0)

    for dx in range(4):
        for dz in range(2):
            p_copy(dx, dz, 1, 1, True).wait_recv()

    both = ((0, 0), (0, 1), (1, 0), (1, 1))
    for t in range(2):
        z_copy(t, 0).wait_send()
        z_copy(t, 1).wait_send()
        for h in range(2):
            for way in range(2):
                y_copy(h, way, t).wait_send()
                f_copy(h, way, t).wait_send()
            for dy in range(4):
                c_copy(h, dy, t).wait_send()
    for t, s in both:
        for dx in range(4):
            for dz in range(2):
                if dx or dz:
                    p_copy(dx, dz, t, s).wait_send()


def last_kernel(done, ops, cols, out, weights, result, sem):
    moves = []
    for c in range(2):
        for o in range(NOP):
            moves.append(pltpu.make_async_copy(done.at[c, o, 0], out.at[c, o, 0], sem.at[c, o, 0]))
            moves.append(pltpu.make_async_copy(done.at[c, o, 1, 0], out.at[c, o, 1, 0], sem.at[c, o, 1]))
    for move in moves:
        move.start()
    real, imag = cols[1, 1, 0], cols[1, 1, 1]
    weights[0:512, 0:512] = real
    weights[0:512, 512:1024] = -imag
    weights[512:1024, 0:512] = imag
    weights[512:1024, 512:1024] = real
    for o in range(NOP):
        for c in range(2):
            for n in range(2):
                rows = slice(512 * c + 256 * n, 512 * c + 256 * n + 256)
                result[c, o, :, 256 * n : 256 * n + 256] = lax.dot_general(
                    ops[1, o], weights[rows, :], (((1,), (1,)), ((), ())), preferred_element_type=jnp.float32
                ).astype(BF16)
            move = pltpu.make_async_copy(result.at[c, o], out.at[c, o, 1, 1], sem.at[c, o, 2])
            move.start()
            moves.append(move)
    for move in moves:
        move.wait()


def shards(perambulator, elementals, op_ids):
    peram = jnp.swapaxes(perambulator, 3, 4)
    dma = pltpu.SemaphoreType.DMA
    vmem = pl.BlockSpec(memory_space=pltpu.VMEM)
    hbm = pl.BlockSpec(memory_space=pl.ANY)
    done, ops, cols = pl.pallas_call(
        kernel,
        out_shape=(
            pltpu.VMEM((2, NOP, 2, 2, 512, 512), BF16),
            pltpu.VMEM((2, NOP, 512, 1024), BF16),
            pltpu.VMEM((2, 2, 2, 512, 512), BF16),
        ),
        in_specs=[pl.BlockSpec(memory_space=pltpu.SMEM), hbm, hbm],
        out_specs=(vmem, vmem, vmem),
        scratch_shapes=[
            pltpu.VMEM((2, 2, 8, 32, 512), BF16),
            pltpu.VMEM((512, 1024), BF16),
            dma(()),
            dma((4, 2, 2, 2)),
            dma((4, 2, 2, 2)),
            dma((2, 2)),
            dma((2, 2)),
            dma((2, 2, 2)),
            dma((2, 2, 2)),
            dma((2, 2, 2)),
            dma((2, 2, 2)),
            dma((2, 4, 2)),
            dma((2, 4, 2)),
        ],
        compiler_params=pltpu.CompilerParams(
            collective_id=0, has_side_effects=True, vmem_limit_bytes=12 * 2**20
        ),
    )(pltpu.with_memory_space_constraint(op_ids, pltpu.HBM), pltpu.with_memory_space_constraint(elementals, pltpu.HBM), pltpu.with_memory_space_constraint(peram, pltpu.HBM))
    return pl.pallas_call(
        last_kernel,
        out_shape=jax.ShapeDtypeStruct((2, NOP, 2, 2, 512, 512), BF16),
        in_specs=[vmem, vmem, vmem],
        out_specs=hbm,
        scratch_shapes=[
            pltpu.VMEM((1024, 1024), BF16),
            pltpu.VMEM((2, NOP, 512, 512), BF16),
            dma((2, NOP, 3)),
        ],
        compiler_params=pltpu.CompilerParams(vmem_limit_bytes=16 * 2**20),
    )(
        pltpu.with_memory_space_constraint(done, pltpu.VMEM),
        pltpu.with_memory_space_constraint(ops, pltpu.VMEM),
        pltpu.with_memory_space_constraint(cols, pltpu.VMEM),
    )


def solution(mesh):
    in_specs = (
        P(None, None, "src", None, "sink"),
        P(None, "sink", None, "src", None),
        P("sink", None),
    )
    out_specs = P(None, None, "sink", "src", None, None)
    return jax.shard_map(shards, mesh=mesh, in_specs=in_specs, out_specs=out_specs, check_vma=False)
```
